32 devices in a mesh: dom: 8 (over z, x), cls: 4 (over y, core).
Axes of the slice: x: 2, y: 2, z: 4, core: 2. Of those that a mesh axis runs over, the one named last changes fastest.
Arguments:
- particles: bfloat16 [256, 16384], P(('dom', 'cls')), may hold values from -6 to 6
- references: bfloat16 [64, 16384], P('cls'), may hold values from -0.046875 to 0.046875
- pose_weights: int32 [256, 24, 64], P(('dom', 'cls')), may hold values from 0 to 4
- class_mask: int32 [256, 64], P(('dom', 'cls')), may hold values 0 or 1
Outputs:
- class_scores: float32 [256, 64], P(('dom', 'cls'))
- class_sums: float32 [64, 16384], P('cls', 'dom')
The draws below stay inside these ranges and needn't reach their ends.
All inputs are finite; a program needn't handle non-finite values. No bound on the sum of `class_mask` on one device may be relied on, other than what follows from the above.
Results may differ from the reference program's by a relative error of at most 0.0003.
Values may be sent and summed in bfloat16 or wider, within the bound.
No kernel may reach another device: no remote copies, remote signals or barrier semaphores. Data moves between devices by JAX's collectives and lax.ppermute only.
A program may use at most 128 MiB of HBM per device.

```python
import math
import jax
import jax.numpy as jnp

CYCLES = 64
ANG = 256
ROT = 24
L = 16384
STEP = 10
K = 64
NPART = 256


def plant(result, stream_key, low, top_value):
    spot = [jax.random.randint(jax.random.fold_in(stream_key, axis), (), 0, length) for axis, length in enumerate(result.shape)]
    widest = result.shape.index(max(result.shape))
    beside = spot[:widest] + [(spot[widest] + 1) % result.shape[widest]] + spot[widest + 1:]
    return result.at[tuple(spot)].set(low).at[tuple(beside)].set(top_value)


def shard_levels(own_key, extent, shards, least, largest):
    gain, own = 1.0, jax.random.fold_in(own_key, 6)
    for dim, shards_of in shards:
        draws = jnp.exp(jax.random.uniform(jax.random.fold_in(own, dim), (shards_of,), jnp.float32, least / len(shards), largest / len(shards)))
        gain = gain * jnp.repeat(draws, extent[dim] // shards_of).reshape([-1 if axis == dim else 1 for axis in range(len(extent))])
    return gain


def scatter_about(stream_key, dims, scale, bound, shards=(), held_as=jnp.bfloat16):
    drawn = jax.random.normal(stream_key, dims, jnp.float32) * scale
    if len(shards) > 0:
        drawn = shard_levels(stream_key, dims, shards, -0.22, 0.18) * drawn
    return jnp.clip(drawn, min=-bound, max=bound).astype(held_as)


def setup_inputs(seed: int = 0) -> dict:
    key_of = jax.random.split(jax.random.key(seed), 5)
    return {
        "particles": scatter_about(key_of[0], (NPART, L), 1.0, 6.0, ((0, 32),)),
        "references": scatter_about(key_of[1], (K, L), L ** -0.5, 0.046875, ((0, 4),)),
        "pose_weights": plant(jax.random.randint(key_of[2], (NPART, ROT, K), 0, 5), jax.random.fold_in(key_of[2], 1), 0, 4).astype(jnp.int32),
        "class_mask": plant((jax.random.randint(key_of[3], (NPART, K), 0, 4) < 3).astype(jnp.int32), jax.random.fold_in(key_of[3], 1), 0, 1),
    }


def turned(images, shift_by):
    shape_in = images.shape
    polar = images.reshape(shape_in[:-1] + (CYCLES, ANG))
    return jnp.roll(polar, shift_by, axis=-1).reshape(shape_in)

def reference(particles, references, pose_weights, class_mask):
    weights = pose_weights * class_mask[:, None, :]
    weights_f = weights.astype(jnp.float32)
    weights_b = weights.astype(jnp.bfloat16)
    scores = jnp.zeros((NPART, K), jnp.float32)
    summed = jnp.zeros((K, L), jnp.float32)
    for r in range(ROT):
        rotated_refs = turned(references, r * STEP)
        corr = jnp.dot(particles, rotated_refs.T, preferred_element_type=jnp.float32)
        scores = scores + weights_f[:, r, :] * corr
        partial_sum = jnp.dot(weights_b[:, r, :].T, particles, preferred_element_type=jnp.float32)
        summed = summed + turned(partial_sum, -r * STEP)
    class_scores = scores / ROT
    class_sums = summed / math.sqrt(NPART * ROT)
    return (class_scores, class_sums)
```

```python
import math

import jax
import jax.numpy as jnp
from jax import lax
from jax.experimental import pallas as pl
from jax.experimental.pallas import tpu as pltpu
from jax.sharding import PartitionSpec as P

CYCLES = 64
ANG = 256
ROT = 24
STEP = ANG // ROT
FINE = 4
COARSE = ROT // FINE
LANES = 128
VMEM_BYTES = 48 * 1024 * 1024
f32 = jnp.float32
bf16 = jnp.bfloat16


def turn(x, shift):
    shift %= ANG
    if shift == 0:
        return x
    halves, rest = shift // LANES, shift % LANES
    lane = lax.broadcasted_iota(jnp.int32, (x.shape[0], LANES), 1)
    pieces = []
    for c in range(x.shape[1] // ANG):
        lo = x[:, c * ANG : c * ANG + LANES]
        hi = x[:, c * ANG + LANES : (c + 1) * ANG]
        if halves:
            lo, hi = hi, lo
        if rest:
            lo, hi = pltpu.roll(lo, rest, 1), pltpu.roll(hi, rest, 1)
            lo, hi = jnp.where(lane < rest, hi, lo), jnp.where(lane < rest, lo, hi)
        pieces += [lo, hi]
    return jnp.concatenate(pieces, axis=1)


def swap_blocks(x, me, block, blocks):
    lane = lax.broadcasted_iota(jnp.int32, x.shape, 1)
    width = x.shape[1]
    bit = 1
    while bit < blocks:
        g = block * bit
        upper = (lane // g) % 2 == 1
        swapped = jnp.where(upper, pltpu.roll(x, g, 1), pltpu.roll(x, width - g, 1))
        x = jnp.where((me // bit) % 2 == 1, swapped, x)
        bit *= 2
    return x


def pack_kernel(part_ref, pose_ref, mask_ref, out_ref):
    dom, n, _ = out_ref.shape
    cols = part_ref.shape[1] // dom
    mask = mask_ref[...]
    for d in range(dom):
        out_ref[d, :, :cols] = part_ref[:, d * cols : (d + 1) * cols]
    for i in range(COARSE):
        w = jnp.concatenate([pose_ref[:, FINE * i + j, :] * mask for j in range(FINE)], axis=1)
        w = w.astype(f32).astype(bf16)
        wide = w.shape[1]
        for d in range(dom):
            out_ref[d, :, cols + i * wide : cols + (i + 1) * wide] = w


def sums_kernel(me_ref, got_ref, keep_ref, send_ref, acc_ref):
    me = me_ref[0]
    groups, per, cols = acc_ref.shape
    k = groups * per
    wide = FINE * k
    dom, n, _ = got_ref.shape
    part = got_ref[:, :, :cols].astype(f32).reshape(dom * n, cols)
    stack = jnp.concatenate([turn(part, -STEP * FINE * i).astype(bf16) for i in range(COARSE)], axis=0)
    w = jnp.concatenate(
        [
            got_ref[:, :, cols + i * wide : cols + (i + 1) * wide].astype(f32).reshape(dom * n, wide).astype(bf16)
            for i in range(COARSE)
        ],
        axis=0,
    )
    total = None
    for j in range(FINE):
        t = lax.dot_general(
            w[:, j * k : (j + 1) * k], stack, (((0,), (0,)), ((), ())), preferred_element_type=f32
        )
        t = turn(t, -STEP * j)
        total = t if total is None else total + t
    acc_ref[...] = total.reshape(groups, per, cols)
    for m in range(groups // 2):
        keep_ref[m] = acc_ref[(2 * m) ^ me]
        send_ref[m] = acc_ref[(2 * m + 1) ^ me]


def scores_kernel(me_ref, part_ref, pose_ref, mask_ref, *refs):
    *blocks, out_ref = refs
    me = me_ref[0]
    n, length = part_ref.shape
    per = blocks[0].shape[0]
    k = per * len(blocks)
    chunk = 4 * ANG
    corr = None
    for c in range(length // chunk):
        at = slice(c * chunk, (c + 1) * chunk)
        part = part_ref[:, at].astype(f32)
        left = jnp.concatenate([turn(part, -STEP * FINE * i) for i in range(COARSE)], axis=0).astype(bf16)
        cls = jnp.concatenate([b[:, at].astype(f32) for b in blocks], axis=0)
        right = jnp.concatenate([turn(cls, STEP * j).astype(bf16) for j in range(FINE)], axis=0)
        more = lax.dot_general(left, right, (((1,), (1,)), ((), ())), preferred_element_type=f32)
        corr = more if corr is None else corr + more
    mask = mask_ref[...]
    total = jnp.zeros((n, FINE * k), f32)
    for i in range(COARSE):
        w = jnp.concatenate([pose_ref[:, FINE * i + j, :] * mask for j in range(FINE)], axis=1).astype(f32)
        total += swap_blocks(w, me, per, len(blocks)) * corr[i * n : (i + 1) * n]
    total = swap_blocks(total, me, per, len(blocks))
    out = total[:, :k]
    for j in range(1, FINE):
        out += total[:, j * k : (j + 1) * k]
    out_ref[...] = out / ROT


def on_device(particles, references, pose_weights, class_mask):
    n, length = particles.shape
    per = references.shape[0]
    k = class_mask.shape[1]
    dom, groups = lax.axis_size("dom"), lax.axis_size("cls")
    cols = length // dom
    me = lax.axis_index("cls").astype(jnp.int32).reshape(1)
    params = pltpu.CompilerParams(vmem_limit_bytes=VMEM_BYTES)
    smem = pl.BlockSpec(memory_space=pltpu.SMEM)
    vmem = pl.BlockSpec(memory_space=pltpu.VMEM)

    def across(x, bit):
        return lax.ppermute(x, "cls", [(c, c ^ bit) for c in range(groups)])

    packed = pl.pallas_call(
        pack_kernel,
        out_shape=jax.ShapeDtypeStruct((dom, n, cols + ROT * k), bf16),
        in_specs=[vmem] * 3,
        out_specs=vmem,
        compiler_params=params,
        name="pack",
    )(particles, pose_weights, class_mask)
    got = lax.all_to_all(packed, "dom", split_axis=0, concat_axis=0, tiled=True)

    blocks = {0: references}
    bit = groups // 2
    while bit:
        blocks.update({s | bit: across(b, bit) for s, b in list(blocks.items())})
        bit //= 2

    keep, send = pl.pallas_call(
        sums_kernel,
        out_shape=[jax.ShapeDtypeStruct((groups // 2, per, cols), f32)] * 2,
        in_specs=[smem, vmem],
        out_specs=[vmem] * 2,
        scratch_shapes=[pltpu.VMEM((groups, per, cols), f32)],
        compiler_params=params,
        name="sums",
    )(me, got)
    bit = 1
    while True:
        keep = keep + across(send, bit)
        bit *= 2
        if bit == groups:
            break
        pairs = keep.reshape(keep.shape[0] // 2, 2, per, cols)
        keep, send = pairs[:, 0], pairs[:, 1]
    particle_total = n * dom * groups
    class_sums = keep[0] / math.sqrt(particle_total * ROT)

    scored = pl.pallas_call(
        scores_kernel,
        out_shape=jax.ShapeDtypeStruct((n, k), f32),
        in_specs=[smem] + [vmem] * (3 + groups),
        out_specs=vmem,
        compiler_params=params,
        name="scores",
    )(me, particles, pose_weights, class_mask, *[blocks[s] for s in range(groups)])
    return (scored, class_sums)


def solution(mesh):
    return jax.shard_map(
        on_device,
        mesh=mesh,
        in_specs=(
            P(("dom", "cls"), None),
            P("cls", None),
            P(("dom", "cls"), None, None),
            P(("dom", "cls"), None),
        ),
        out_specs=(P(("dom", "cls"), None), P("cls", "dom")),
        check_vma=False,
    )
```

```python
import math

import jax
import jax.numpy as jnp
from jax import lax
from jax.experimental import pallas as pl
from jax.experimental.pallas import tpu as pltpu
from jax.sharding import PartitionSpec as P

CYCLES = 64
ANG = 256
ROT = 24
STEP = ANG // ROT
FINE = 4
COARSE = ROT // FINE
PAIR = 2
CHUNK = 4
LANES = 128
VMEM_BYTES = 48 * 1024 * 1024
VMEM_MOST = 66584576
f32 = jnp.float32
bf16 = jnp.bfloat16


def turn(x, shift):
    shift %= ANG
    if shift == 0:
        return x
    halves, rest = shift // LANES, shift % LANES
    lane = lax.broadcasted_iota(jnp.int32, (x.shape[0], LANES), 1)
    pieces = []
    for c in range(x.shape[1] // ANG):
        lo = x[:, c * ANG : c * ANG + LANES]
        hi = x[:, c * ANG + LANES : (c + 1) * ANG]
        if halves:
            lo, hi = hi, lo
        if rest:
            lo, hi = pltpu.roll(lo, rest, 1), pltpu.roll(hi, rest, 1)
            lo, hi = jnp.where(lane < rest, hi, lo), jnp.where(lane < rest, lo, hi)
        pieces += [lo, hi]
    return jnp.concatenate(pieces, axis=1)


def swap_blocks(x, me, block, blocks):
    lane = lax.broadcasted_iota(jnp.int32, x.shape, 1)
    width = x.shape[1]
    bit = 1
    while bit < blocks:
        g = block * bit
        upper = (lane // g) % 2 == 1
        swapped = jnp.where(upper, pltpu.roll(x, g, 1), pltpu.roll(x, width - g, 1))
        x = jnp.where((me // bit) % 2 == 1, swapped, x)
        bit *= 2
    return x


def pack_kernel(part_hbm, pose_hbm, mask_hbm, out_ref, weights_ref, pose_ref, mask_ref, sems):
    dom, _, _ = out_ref.shape
    cols = part_hbm.shape[1] // dom
    me, groups = lax.axis_index("cls"), lax.axis_size("cls")
    k = pose_ref.shape[2]
    half = k // 2
    wide = FINE * k
    small = [
        pltpu.make_async_copy(pose_hbm, pose_ref, sems.at[dom]),
        pltpu.make_async_copy(mask_hbm, mask_ref, sems.at[dom + 1]),
    ]
    large = [
        pltpu.make_async_copy(
            part_hbm.at[:, pl.ds(d * cols, cols)], out_ref.at[d, :, pl.ds(0, cols)], sems.at[d]
        )
        for d in range(dom)
    ]
    for copy in small + large:
        copy.start()
    for copy in small:
        copy.wait()
    mask = mask_ref[...]
    for i in range(COARSE):
        fine = [pose_ref[:, FINE * i + j, :] * mask for j in range(FINE)]
        w = swap_blocks(jnp.concatenate(fine, axis=1).astype(f32), me, k // groups, groups)
        pieces = [w[:, j * k + h * half : j * k + (h + 1) * half] for h in range(2) for j in range(FINE)]
        w = jnp.concatenate(pieces, axis=1).astype(bf16)
        weights_ref[:, i * wide : (i + 1) * wide] = w
        for d in range(dom):
            out_ref[d, :, cols + i * wide : cols + (i + 1) * wide] = w
    for copy in large:
        copy.wait()


def half_sums(got_ref, stack, half):
    dom, n, width = got_ref.shape
    cols = stack.shape[1]
    wide = (width - cols) // COARSE // 2
    k = wide // FINE
    rows = []
    for i in range(COARSE):
        first = cols + (2 * i + half) * wide
        rows.append(got_ref[:, :, first : first + wide].astype(f32).reshape(dom * n, wide))
    w = jnp.concatenate(rows, axis=0).astype(bf16)
    t = lax.dot_general(w, stack, (((0,), (0,)), ((), ())), preferred_element_type=f32)
    total = t[:k]
    for j in range(1, FINE):
        total = total + turn(t[j * k : (j + 1) * k], -STEP * j)
    return total


def put_pairs(total, keep_ref, send_ref):
    half, per, _ = keep_ref.shape
    for m in range(half):
        keep_ref[m] = total[2 * m * per : (2 * m + 1) * per]
        if total.shape[0] > per:
            send_ref[m] = total[(2 * m + 1) * per : (2 * m + 2) * per]


def far_sums_kernel(got_ref, stack_ref, keep_ref, send_ref):
    dom, n, _ = got_ref.shape
    cols = stack_ref.shape[1]
    part = got_ref[:, :, :cols].astype(f32).reshape(dom * n, cols)
    stack = jnp.concatenate([turn(part, -STEP * FINE * i).astype(bf16) for i in range(COARSE)], axis=0)
    stack_ref[...] = stack
    put_pairs(half_sums(got_ref, stack, 1), keep_ref, send_ref)


def near_sums_kernel(got_ref, stack_ref, keep_ref, send_ref):
    put_pairs(half_sums(got_ref, stack_ref[...], 0), keep_ref, send_ref)


def half_scores(part_ref, weights_ref, blocks, half):
    n, length = part_ref.shape
    k = blocks[0].shape[0] * len(blocks)
    chunk = CHUNK * ANG
    corr = None
    for c in range(length // chunk):
        at = slice(c * chunk, (c + 1) * chunk)
        part = part_ref[:, at].astype(f32)
        left = jnp.concatenate([turn(part, -STEP * PAIR * m) for m in range(ROT // PAIR)], axis=0).astype(bf16)
        cls = jnp.concatenate([b[:, at].astype(f32) for b in blocks], axis=0)
        right = jnp.concatenate([turn(cls, STEP * j).astype(bf16) for j in range(PAIR)], axis=0)
        more = lax.dot_general(left, right, (((1,), (1,)), ((), ())), preferred_element_type=f32)
        corr = more if corr is None else corr + more
    wide = PAIR * k
    total = None
    for m in range(ROT // PAIR):
        i, b = m // 2, m % 2
        first = ((2 * i + half) * 2 + b) * wide
        w = weights_ref[:, first : first + wide].astype(f32)
        more = w * corr[m * n : (m + 1) * n]
        total = more if total is None else total + more
    out = total[:, :k]
    for j in range(1, PAIR):
        out = out + total[:, j * k : (j + 1) * k]
    return out


def near_scores_kernel(part_ref, weights_ref, *refs):
    *blocks, out_ref = refs
    out_ref[...] = half_scores(part_ref, weights_ref, blocks, 0)


def far_scores_kernel(near_ref, part_ref, weights_ref, *refs):
    *blocks, out_ref = refs
    groups = lax.axis_size("cls")
    far = half_scores(part_ref, weights_ref, blocks, 1)
    out = jnp.concatenate([near_ref[...], far], axis=1)
    out_ref[...] = swap_blocks(out, lax.axis_index("cls"), out.shape[1] // groups, groups) / ROT


def on_device(particles, references, pose_weights, class_mask):
    n, length = particles.shape
    per = references.shape[0]
    k = class_mask.shape[1]
    dom, groups = lax.axis_size("dom"), lax.axis_size("cls")
    cols = length // dom
    last = groups // 2
    hbm = pl.BlockSpec(memory_space=pl.ANY)
    vmem = pl.BlockSpec(memory_space=pltpu.VMEM)

    def call(kernel, name, outs, ins, scratch=(), limit=VMEM_BYTES):
        return pl.pallas_call(
            kernel,
            out_shape=[jax.ShapeDtypeStruct(*o) for o in outs],
            in_specs=ins,
            out_specs=[vmem] * len(outs),
            scratch_shapes=list(scratch),
            compiler_params=pltpu.CompilerParams(vmem_limit_bytes=limit),
            name=name,
        )

    def after(x, other):
        return lax.optimization_barrier((x, other))[0]

    def across(x, bit):
        return lax.ppermute(x, "cls", [(c, c ^ bit) for c in range(groups)])

    def reduced(keep, send):
        bit = 1
        while bit < last:
            keep = keep + across(send, bit)
            bit *= 2
            if bit < last:
                pairs = keep.reshape(keep.shape[0] // 2, 2, per, cols)
                keep, send = pairs[:, 0], pairs[:, 1]
        return keep[0]

    packed, weights = call(
        pack_kernel,
        "pack",
        [((dom, n, cols + ROT * k), bf16), ((n, ROT * k), bf16)],
        [hbm] * 3,
        [
            pltpu.VMEM(pose_weights.shape, jnp.int32),
            pltpu.VMEM(class_mask.shape, jnp.int32),
            pltpu.SemaphoreType.DMA((dom + 2,)),
        ],
        VMEM_MOST,
    )(particles, pose_weights, class_mask)
    got = lax.all_to_all(packed, "dom", split_axis=0, concat_axis=0, tiled=True)
    blocks = {0: references}
    bit = last
    while bit:
        for s, b in list(blocks.items()):
            blocks[s | bit] = across(after(b, packed) if s == 0 else b, bit)
        bit //= 2
    near, far = [blocks[s] for s in range(last)], [blocks[s] for s in range(last, groups)]
    (near_scores,) = call(
        near_scores_kernel, "near_scores", [((n, k // 2), f32)], [vmem] * (2 + last)
    )(particles, weights, *near)
    got = after(got, near_scores)

    send_shape = (max(last // 2, 1), per, cols)
    stack, keep, send = call(
        far_sums_kernel,
        "far_sums",
        [((n * dom * COARSE, cols), bf16), (send_shape, f32), (send_shape, f32)],
        [vmem],
    )(got)
    leaving = reduced(keep, send)
    arriving = across(leaving, last)
    stack = after(stack, leaving)

    keep, send = call(near_sums_kernel, "near_sums", [(send_shape, f32)] * 2, [vmem] * 2)(got, stack)
    near_sums = reduced(keep, send)

    (scored,) = call(far_scores_kernel, "far_scores", [((n, k), f32)], [vmem] * (3 + last))(
        near_scores, particles, weights, *far
    )
    arriving = after(arriving, scored)
    class_sums = (near_sums + arriving) / math.sqrt(n * dom * groups * ROT)
    return (scored, class_sums)


def solution(mesh):
    return jax.shard_map(
        on_device,
        mesh=mesh,
        in_specs=(
            P(("dom", "cls"), None),
            P("cls", None),
            P(("dom", "cls"), None, None),
            P(("dom", "cls"), None),
        ),
        out_specs=(P(("dom", "cls"), None), P("cls", "dom")),
        check_vma=False,
    )
```

```python
import functools
import math

import jax
import jax.numpy as jnp
from jax import lax
from jax.experimental import pallas as pl
from jax.experimental.pallas import tpu as pltpu
from jax.sharding import PartitionSpec as P

CYCLES = 64
ANG = 256
ROT = 24
STEP = ANG // ROT
FINE = 4
COARSE = ROT // FINE
PAIR = 2
CHUNK = 4
LANES = 128
VMEM_BYTES = 48 * 1024 * 1024
VMEM_MOST = 65900000
f32 = jnp.float32
bf16 = jnp.bfloat16


def turn(x, shift):
    shift %= ANG
    if shift == 0:
        return x
    halves, rest = shift // LANES, shift % LANES
    lane = lax.broadcasted_iota(jnp.int32, (x.shape[0], LANES), 1)
    pieces = []
    for c in range(x.shape[1] // ANG):
        lo = x[:, c * ANG : c * ANG + LANES]
        hi = x[:, c * ANG + LANES : (c + 1) * ANG]
        if halves:
            lo, hi = hi, lo
        if rest:
            lo, hi = pltpu.roll(lo, rest, 1), pltpu.roll(hi, rest, 1)
            lo, hi = jnp.where(lane < rest, hi, lo), jnp.where(lane < rest, lo, hi)
        pieces += [lo, hi]
    return jnp.concatenate(pieces, axis=1)


def swap_blocks(x, me, block, blocks):
    lane = lax.broadcasted_iota(jnp.int32, x.shape, 1)
    width = x.shape[1]
    bit = 1
    while bit < blocks:
        g = block * bit
        upper = (lane // g) % 2 == 1
        swapped = jnp.where(upper, pltpu.roll(x, g, 1), pltpu.roll(x, width - g, 1))
        x = jnp.where((me // bit) % 2 == 1, swapped, x)
        bit *= 2
    return x


def pack_kernel(part_hbm, pose_hbm, mask_hbm, *refs):
    slots, (pose_ref, mask_ref, sems) = refs[:-3], refs[-3:]
    dom = len(slots)
    cols = part_hbm.shape[1] // dom
    d, me, groups = lax.axis_index("dom"), lax.axis_index("cls"), lax.axis_size("cls")
    k = pose_ref.shape[2]
    half = k // 2
    small = [
        pltpu.make_async_copy(pose_hbm, pose_ref, sems.at[dom]),
        pltpu.make_async_copy(mask_hbm, mask_ref, sems.at[dom + 1]),
    ]
    large = [
        pltpu.make_async_copy(
            part_hbm.at[:, pl.ds(pl.multiple_of((d ^ s) * cols, cols), cols)],
            slots[s].at[:, pl.ds(0, cols)],
            sems.at[s],
        )
        for s in range(dom)
    ]
    for copy in small + large:
        copy.start()
    for copy in small:
        copy.wait()
    mask = mask_ref[...]
    for i in range(COARSE):
        fine = [pose_ref[:, FINE * i + j, :] * mask for j in range(FINE)]
        w = swap_blocks(jnp.concatenate(fine, axis=1).astype(f32), me, k // groups, groups)
        pieces = [w[:, j * k + h * half : j * k + (h + 1) * half] for h in range(2) for j in range(FINE)]
        w = jnp.concatenate(pieces, axis=1).astype(bf16)
        wide = w.shape[1]
        for slot in slots:
            slot[:, cols + i * wide : cols + (i + 1) * wide] = w
    for copy in large:
        copy.wait()


def rows_of(got, at):
    return jnp.concatenate([g[:, at].astype(f32) for g in got], axis=0)


def half_sums(got, stack, half):
    cols = stack.shape[1]
    wide = (got[0].shape[1] - cols) // COARSE // 2
    k = wide // FINE
    at = [slice(cols + (2 * i + half) * wide, cols + (2 * i + half + 1) * wide) for i in range(COARSE)]
    w = jnp.concatenate([rows_of(got, a).astype(bf16) for a in at], axis=0)
    t = lax.dot_general(w, stack, (((0,), (0,)), ((), ())), preferred_element_type=f32)
    total = t[:k]
    for j in range(1, FINE):
        total = total + turn(t[j * k : (j + 1) * k], -STEP * j)
    return total


def put_pairs(total, keep_ref, send_ref):
    half, per, _ = keep_ref.shape
    for m in range(half):
        keep_ref[m] = total[2 * m * per : (2 * m + 1) * per]
        if total.shape[0] > per:
            send_ref[m] = total[(2 * m + 1) * per : (2 * m + 2) * per]


def far_sums_kernel(count, *refs):
    got, (stack_ref, *outs) = refs[:count], refs[-3:]
    cols = stack_ref.shape[1]
    part = rows_of(got, slice(0, cols))
    stack = jnp.concatenate([turn(part, -STEP * FINE * i).astype(bf16) for i in range(COARSE)], axis=0)
    stack_ref[...] = stack
    put_pairs(half_sums(got, stack, 1), *outs)


def near_sums_kernel(count, stack_ref, *refs):
    got, (keep_ref, send_ref) = refs[:count], refs[-2:]
    put_pairs(half_sums(got, stack_ref[...], 0), keep_ref, send_ref)


def correlate(part_ref, blocks):
    length = part_ref.shape[1]
    chunk = CHUNK * ANG
    corr = None
    for c in range(length // chunk):
        at = slice(c * chunk, (c + 1) * chunk)
        part = part_ref[:, at].astype(f32)
        left = jnp.concatenate([turn(part, -STEP * PAIR * m) for m in range(ROT // PAIR)], axis=0).astype(bf16)
        cls = jnp.concatenate([b[:, at].astype(f32) for b in blocks], axis=0)
        right = jnp.concatenate([turn(cls, STEP * j).astype(bf16) for j in range(PAIR)], axis=0)
        more = lax.dot_general(left, right, (((1,), (1,)), ((), ())), preferred_element_type=f32)
        corr = more if corr is None else corr + more
    return corr


def weighted(corr, weights_ref, half):
    n = weights_ref.shape[0]
    wide = corr.shape[1]
    k = wide // PAIR
    cols = weights_ref.shape[1] - ROT * 2 * k
    total = None
    for m in range(ROT // PAIR):
        i, b = m // 2, m % 2
        first = cols + ((2 * i + half) * 2 + b) * wide
        w = weights_ref[:, first : first + wide].astype(f32)
        more = w * corr[m * n : (m + 1) * n]
        total = more if total is None else total + more
    out = total[:, :k]
    for j in range(1, PAIR):
        out = out + total[:, j * k : (j + 1) * k]
    return out


def guest_kernel(part_ref, packed_ref, *refs):
    *blocks, out_ref, own_ref = refs
    out_ref[...] = correlate(part_ref, blocks)
    own_ref[...] = packed_ref[...]


def near_scores_kernel(part_ref, weights_ref, *refs):
    *blocks, out_ref = refs
    out_ref[...] = weighted(correlate(part_ref, blocks), weights_ref, 0)


def scores_kernel(near_ref, back_ref, weights_ref, out_ref):
    groups = lax.axis_size("cls")
    far = weighted(back_ref[...], weights_ref, 1)
    out = jnp.concatenate([near_ref[...], far], axis=1)
    out_ref[...] = swap_blocks(out, lax.axis_index("cls"), out.shape[1] // groups, groups) / ROT


def on_device(particles, references, pose_weights, class_mask):
    n, length = particles.shape
    per = references.shape[0]
    k = class_mask.shape[1]
    dom, groups = lax.axis_size("dom"), lax.axis_size("cls")
    cols = length // dom
    last = groups // 2
    hbm = pl.BlockSpec(memory_space=pl.ANY)
    vmem = pl.BlockSpec(memory_space=pltpu.VMEM)

    def call(kernel, name, outs, ins, scratch=(), limit=VMEM_BYTES, cost=None):
        return pl.pallas_call(
            kernel,
            out_shape=[jax.ShapeDtypeStruct(*o) for o in outs],
            in_specs=ins,
            out_specs=[vmem] * len(outs),
            scratch_shapes=list(scratch),
            compiler_params=pltpu.CompilerParams(vmem_limit_bytes=limit),
            name=name,
            cost_estimate=cost,
        )

    def after(x, other):
        return lax.optimization_barrier((x, other))[0]

    def across(x, bit):
        return lax.ppermute(x, "cls", [(c, c ^ bit) for c in range(groups)])

    def reduced(keep, send):
        bit = 1
        while bit < last:
            keep = keep + across(send, bit)
            bit *= 2
            if bit < last:
                pairs = keep.reshape(keep.shape[0] // 2, 2, per, cols)
                keep, send = pairs[:, 0], pairs[:, 1]
        return keep[0]

    blocks = {0: references}
    bit = last // 2
    while bit:
        blocks.update({s | bit: across(b, bit) for s, b in list(blocks.items())})
        bit //= 2
    near = [blocks[s] for s in range(last)]
    packed = call(
        pack_kernel,
        "pack",
        [((n, cols + ROT * k), bf16)] * dom,
        [hbm] * 3,
        [
            pltpu.VMEM(pose_weights.shape, jnp.int32),
            pltpu.VMEM(class_mask.shape, jnp.int32),
            pltpu.SemaphoreType.DMA((dom + 2,)),
        ],
        VMEM_MOST,
    )(particles, pose_weights, class_mask)
    guests = across(after(particles, packed), last)
    packed = after(packed, near)
    got = [packed[0]]
    for s in range(dom - 1, 0, -1):
        x = packed[s]
        got.append(lax.ppermute(x, "dom", [(d, d ^ s) for d in range(dom)]))

    back, got[0] = call(
        guest_kernel,
        "guest_scores",
        [((n * ROT // PAIR, PAIR * k // 2), f32), (packed[0].shape, bf16)],
        [vmem] * (2 + last),
    )(guests, packed[0], *near)
    got = after(got, back)
    send_shape = (max(last // 2, 1), per, cols)
    stack, keep, send = call(
        functools.partial(far_sums_kernel, dom),
        "far_sums",
        [((n * dom * COARSE, cols), bf16), (send_shape, f32), (send_shape, f32)],
        [vmem] * dom,
    )(*got)
    back = across(after(back, send), last)
    leaving = reduced(keep, send)
    arriving = across(leaving, last)
    (near_scores,) = call(near_scores_kernel, "near_scores", [((n, k // 2), f32)], [vmem] * (2 + last))(
        after(particles, leaving), got[0], *near
    )
    stack = after(stack, (near_scores, back))

    keep, send = call(
        functools.partial(near_sums_kernel, dom), "near_sums", [(send_shape, f32)] * 2, [vmem] * (1 + dom)
    )(stack, *got)
    near_sums = reduced(keep, send)

    (scored,) = call(scores_kernel, "scores", [((n, k), f32)], [vmem] * 3)(near_scores, back, got[0])
    arriving = after(arriving, scored)
    class_sums = (near_sums + arriving) / math.sqrt(n * dom * groups * ROT)
    return (scored, class_sums)


def solution(mesh):
    return jax.shard_map(
        on_device,
        mesh=mesh,
        in_specs=(
            P(("dom", "cls"), None),
            P("cls", None),
            P(("dom", "cls"), None, None),
            P(("dom", "cls"), None),
        ),
        out_specs=(P(("dom", "cls"), None), P("cls", "dom")),
        check_vma=False,
    )
```

```python
import functools
import math

import jax
import jax.numpy as jnp
from jax import lax
from jax.experimental import pallas as pl
from jax.experimental.pallas import tpu as pltpu
from jax.sharding import PartitionSpec as P

CYCLES = 64
ANG = 256
ROT = 24
STEP = ANG // ROT
FINE = 4
COARSE = ROT // FINE
PAIR = 2
CHUNK = 4
LANES = 128
VMEM_BYTES = 48 * 1024 * 1024
VMEM_MOST = 65900000
f32 = jnp.float32
bf16 = jnp.bfloat16


def turn(x, shift):
    shift %= ANG
    if shift == 0:
        return x
    halves, rest = shift // LANES, shift % LANES
    lane = lax.broadcasted_iota(jnp.int32, (x.shape[0], LANES), 1)
    pieces = []
    for c in range(x.shape[1] // ANG):
        lo = x[:, c * ANG : c * ANG + LANES]
        hi = x[:, c * ANG + LANES : (c + 1) * ANG]
        if halves:
            lo, hi = hi, lo
        if rest:
            lo, hi = pltpu.roll(lo, rest, 1), pltpu.roll(hi, rest, 1)
            lo, hi = jnp.where(lane < rest, hi, lo), jnp.where(lane < rest, lo, hi)
        pieces += [lo, hi]
    return jnp.concatenate(pieces, axis=1)


def swap_blocks(x, me, block, blocks):
    lane = lax.broadcasted_iota(jnp.int32, x.shape, 1)
    width = x.shape[1]
    bit = 1
    while bit < blocks:
        g = block * bit
        upper = (lane // g) % 2 == 1
        swapped = jnp.where(upper, pltpu.roll(x, g, 1), pltpu.roll(x, width - g, 1))
        x = jnp.where((me // bit) % 2 == 1, swapped, x)
        bit *= 2
    return x


def pack_kernel(part_hbm, pose_hbm, mask_hbm, *refs):
    slots, (pose_ref, mask_ref, sems) = refs[:-3], refs[-3:]
    dom = len(slots)
    cols = part_hbm.shape[1] // dom
    d, me, groups = lax.axis_index("dom"), lax.axis_index("cls"), lax.axis_size("cls")
    k = pose_ref.shape[2]
    half = k // 2
    small = [
        pltpu.make_async_copy(pose_hbm, pose_ref, sems.at[dom]),
        pltpu.make_async_copy(mask_hbm, mask_ref, sems.at[dom + 1]),
    ]
    large = [
        pltpu.make_async_copy(
            part_hbm.at[:, pl.ds(pl.multiple_of((d ^ s) * cols, cols), cols)],
            slots[s].at[:, pl.ds(0, cols)],
            sems.at[s],
        )
        for s in range(dom)
    ]
    for copy in small + large:
        copy.start()
    for copy in small:
        copy.wait()
    mask = mask_ref[...]
    for i in range(COARSE):
        fine = [pose_ref[:, FINE * i + j, :] * mask for j in range(FINE)]
        w = swap_blocks(jnp.concatenate(fine, axis=1).astype(f32), me, k // groups, groups)
        pieces = [w[:, j * k + h * half : j * k + (h + 1) * half] for h in range(2) for j in range(FINE)]
        w = jnp.concatenate(pieces, axis=1).astype(bf16)
        wide = w.shape[1]
        for slot in slots:
            slot[:, cols + i * wide : cols + (i + 1) * wide] = w
    for copy in large:
        copy.wait()


def rows_of(got, at):
    return jnp.concatenate([g[:, at].astype(f32) for g in got], axis=0)


def half_sums(got, stack, half):
    cols = stack.shape[1]
    wide = (got[0].shape[1] - cols) // COARSE // 2
    k = wide // FINE
    at = [slice(cols + (2 * i + half) * wide, cols + (2 * i + half + 1) * wide) for i in range(COARSE)]
    w = jnp.concatenate([rows_of(got, a).astype(bf16) for a in at], axis=0)
    t = lax.dot_general(w, stack, (((0,), (0,)), ((), ())), preferred_element_type=f32)
    total = t[:k]
    for j in range(1, FINE):
        total = total + turn(t[j * k : (j + 1) * k], -STEP * j)
    return total


def put_pairs(total, keep_ref, send_ref):
    half, per, _ = keep_ref.shape
    for m in range(half):
        keep_ref[m] = total[2 * m * per : (2 * m + 1) * per]
        if total.shape[0] > per:
            send_ref[m] = total[(2 * m + 1) * per : (2 * m + 2) * per]


def far_sums_kernel(count, *refs):
    got, (stack_ref, *outs) = refs[:count], refs[-3:]
    cols = stack_ref.shape[1]
    part = rows_of(got, slice(0, cols))
    stack = jnp.concatenate([turn(part, -STEP * FINE * i).astype(bf16) for i in range(COARSE)], axis=0)
    stack_ref[...] = stack
    put_pairs(half_sums(got, stack, 1), *outs)


def near_sums_kernel(count, stack_ref, *refs):
    got, (keep_ref, send_ref) = refs[:count], refs[-2:]
    put_pairs(half_sums(got, stack_ref[...], 0), keep_ref, send_ref)


def correlate(part_ref, blocks):
    length = part_ref.shape[1]
    chunk = CHUNK * ANG
    corr = None
    for c in range(length // chunk):
        at = slice(c * chunk, (c + 1) * chunk)
        part = part_ref[:, at].astype(f32)
        left = jnp.concatenate([turn(part, -STEP * PAIR * m) for m in range(ROT // PAIR)], axis=0).astype(bf16)
        cls = jnp.concatenate([b[:, at].astype(f32) for b in blocks], axis=0)
        right = jnp.concatenate([turn(cls, STEP * j).astype(bf16) for j in range(PAIR)], axis=0)
        more = lax.dot_general(left, right, (((1,), (1,)), ((), ())), preferred_element_type=f32)
        corr = more if corr is None else corr + more
    return corr


def weighted(corr, weights_ref, half):
    n = weights_ref.shape[0]
    wide = corr.shape[1]
    k = wide // PAIR
    cols = weights_ref.shape[1] - ROT * 2 * k
    total = None
    for m in range(ROT // PAIR):
        i, b = m // 2, m % 2
        first = cols + ((2 * i + half) * 2 + b) * wide
        w = weights_ref[:, first : first + wide].astype(f32)
        more = w * corr[m * n : (m + 1) * n]
        total = more if total is None else total + more
    out = total[:, :k]
    for j in range(1, PAIR):
        out = out + total[:, j * k : (j + 1) * k]
    return out


def guest_kernel(part_ref, packed_ref, *refs):
    *blocks, out_ref, own_ref = refs
    out_ref[...] = correlate(part_ref, blocks)
    own_ref[...] = packed_ref[...]


def near_scores_kernel(part_ref, weights_ref, *refs):
    *blocks, out_ref = refs
    out_ref[...] = weighted(correlate(part_ref, blocks), weights_ref, 0)


def scores_kernel(near_ref, back_ref, weights_ref, out_ref):
    groups = lax.axis_size("cls")
    far = weighted(back_ref[...], weights_ref, 1)
    out = jnp.concatenate([near_ref[...], far], axis=1)
    out_ref[...] = swap_blocks(out, lax.axis_index("cls"), out.shape[1] // groups, groups) / ROT


def on_device(particles, references, pose_weights, class_mask):
    n, length = particles.shape
    per = references.shape[0]
    k = class_mask.shape[1]
    dom, groups = lax.axis_size("dom"), lax.axis_size("cls")
    cols = length // dom
    last = groups // 2
    hbm = pl.BlockSpec(memory_space=pl.ANY)
    vmem = pl.BlockSpec(memory_space=pltpu.VMEM)

    def call(kernel, name, outs, ins, scratch=(), limit=VMEM_BYTES, cost=None):
        return pl.pallas_call(
            kernel,
            out_shape=[jax.ShapeDtypeStruct(*o) for o in outs],
            in_specs=ins,
            out_specs=[vmem] * len(outs),
            scratch_shapes=list(scratch),
            compiler_params=pltpu.CompilerParams(vmem_limit_bytes=limit),
            name=name,
            cost_estimate=cost,
        )

    def after(x, other):
        return lax.optimization_barrier((x, other))[0]

    def across(x, bit):
        return lax.ppermute(x, "cls", [(c, c ^ bit) for c in range(groups)])

    def reduced(keep, send):
        bit = 1
        while bit < last:
            keep = keep + across(send, bit)
            bit *= 2
            if bit < last:
                pairs = keep.reshape(keep.shape[0] // 2, 2, per, cols)
                keep, send = pairs[:, 0], pairs[:, 1]
        return keep[0]

    blocks = {0: references}
    bit = last // 2
    while bit:
        blocks.update({s | bit: across(b, bit) for s, b in list(blocks.items())})
        bit //= 2
    near = [blocks[s] for s in range(last)]
    packed = call(
        pack_kernel,
        "pack",
        [((n, cols + ROT * k), bf16)] * dom,
        [hbm] * 3,
        [
            pltpu.VMEM(pose_weights.shape, jnp.int32),
            pltpu.VMEM(class_mask.shape, jnp.int32),
            pltpu.SemaphoreType.DMA((dom + 2,)),
        ],
        VMEM_MOST,
    )(particles, pose_weights, class_mask)
    packed = after(packed, near)
    got = [packed[0]]
    for s in range(dom - 1, 0, -1):
        x = packed[s]
        got.append(lax.ppermute(x, "dom", [(d, d ^ s) for d in range(dom)]))

    guests = across(particles, last)
    back, got[0] = call(
        guest_kernel,
        "guest_scores",
        [((n * ROT // PAIR, PAIR * k // 2), f32), (packed[0].shape, bf16)],
        [vmem] * (2 + last),
    )(guests, packed[0], *near)
    got = after(got, back)
    send_shape = (max(last // 2, 1), per, cols)
    stack, keep, send = call(
        functools.partial(far_sums_kernel, dom),
        "far_sums",
        [((n * dom * COARSE, cols), bf16), (send_shape, f32), (send_shape, f32)],
        [vmem] * dom,
    )(*got)
    back = across(after(back, send), last)
    leaving = reduced(keep, send)
    arriving = across(leaving, last)
    (near_scores,) = call(near_scores_kernel, "near_scores", [((n, k // 2), f32)], [vmem] * (2 + last))(
        after(particles, leaving), got[0], *near
    )
    stack = after(stack, (near_scores, back))

    keep, send = call(
        functools.partial(near_sums_kernel, dom), "near_sums", [(send_shape, f32)] * 2, [vmem] * (1 + dom)
    )(stack, *got)
    near_sums = reduced(keep, send)

    (scored,) = call(scores_kernel, "scores", [((n, k), f32)], [vmem] * 3)(near_scores, back, got[0])
    arriving = after(arriving, scored)
    class_sums = (near_sums + arriving) / math.sqrt(n * dom * groups * ROT)
    return (scored, class_sums)


def solution(mesh):
    return jax.shard_map(
        on_device,
        mesh=mesh,
        in_specs=(
            P(("dom", "cls"), None),
            P("cls", None),
            P(("dom", "cls"), None, None),
            P(("dom", "cls"), None),
        ),
        out_specs=(P(("dom", "cls"), None), P("cls", "dom")),
        check_vma=False,
    )
```

```python
import functools
import math

import jax
import jax.numpy as jnp
from jax import lax
from jax.experimental import pallas as pl
from jax.experimental.pallas import tpu as pltpu
from jax.sharding import PartitionSpec as P

CYCLES = 64
ANG = 256
ROT = 24
STEP = ANG // ROT
FINE = 4
COARSE = ROT // FINE
PAIR = 2
CHUNK = 4
LANES = 128
VMEM_BYTES = 48 * 1024 * 1024
VMEM_MOST = 65900000
f32 = jnp.float32
bf16 = jnp.bfloat16


def turn(x, shift):
    shift %= ANG
    if shift == 0:
        return x
    halves, rest = shift // LANES, shift % LANES
    lane = lax.broadcasted_iota(jnp.int32, (x.shape[0], LANES), 1)
    pieces = []
    for c in range(x.shape[1] // ANG):
        lo = x[:, c * ANG : c * ANG + LANES]
        hi = x[:, c * ANG + LANES : (c + 1) * ANG]
        if halves:
            lo, hi = hi, lo
        if rest:
            lo, hi = pltpu.roll(lo, rest, 1), pltpu.roll(hi, rest, 1)
            lo, hi = jnp.where(lane < rest, hi, lo), jnp.where(lane < rest, lo, hi)
        pieces += [lo, hi]
    return jnp.concatenate(pieces, axis=1)


def swap_blocks(x, me, block, blocks):
    lane = lax.broadcasted_iota(jnp.int32, x.shape, 1)
    width = x.shape[1]
    bit = 1
    while bit < blocks:
        g = block * bit
        upper = (lane // g) % 2 == 1
        swapped = jnp.where(upper, pltpu.roll(x, g, 1), pltpu.roll(x, width - g, 1))
        x = jnp.where((me // bit) % 2 == 1, swapped, x)
        bit *= 2
    return x


def pack_kernel(part_ref, pose_ref, mask_ref, *slots):
    cols = part_ref.shape[1] // len(slots)
    d, me, groups = lax.axis_index("dom"), lax.axis_index("cls"), lax.axis_size("cls")
    k = pose_ref.shape[2]
    half = k // 2
    for s, slot in enumerate(slots):
        slot[:, :cols] = part_ref[:, pl.ds(pl.multiple_of((d ^ s) * cols, cols), cols)]
    mask = mask_ref[...]
    for i in range(COARSE):
        fine = [pose_ref[:, FINE * i + j, :] * mask for j in range(FINE)]
        w = swap_blocks(jnp.concatenate(fine, axis=1).astype(f32), me, k // groups, groups)
        pieces = [w[:, j * k + h * half : j * k + (h + 1) * half] for h in range(2) for j in range(FINE)]
        w = jnp.concatenate(pieces, axis=1).astype(bf16)
        wide = w.shape[1]
        for slot in slots:
            slot[:, cols + i * wide : cols + (i + 1) * wide] = w


def rows_of(got, at):
    return jnp.concatenate([g[:, at].astype(f32) for g in got], axis=0)


def half_sums(got, stack, half):
    cols = stack.shape[1]
    wide = (got[0].shape[1] - cols) // COARSE // 2
    k = wide // FINE
    at = [slice(cols + (2 * i + half) * wide, cols + (2 * i + half + 1) * wide) for i in range(COARSE)]
    w = jnp.concatenate([rows_of(got, a).astype(bf16) for a in at], axis=0)
    t = lax.dot_general(w, stack, (((0,), (0,)), ((), ())), preferred_element_type=f32)
    total = t[:k]
    for j in range(1, FINE):
        total = total + turn(t[j * k : (j + 1) * k], -STEP * j)
    return total


def put_pairs(total, keep_ref, send_ref):
    half, per, _ = keep_ref.shape
    for m in range(half):
        keep_ref[m] = total[2 * m * per : (2 * m + 1) * per]
        if total.shape[0] > per:
            send_ref[m] = total[(2 * m + 1) * per : (2 * m + 2) * per]


def far_sums_kernel(count, *refs):
    got, (stack_ref, *outs) = refs[:count], refs[-3:]
    cols = stack_ref.shape[1]
    part = rows_of(got, slice(0, cols))
    stack = jnp.concatenate([turn(part, -STEP * FINE * i).astype(bf16) for i in range(COARSE)], axis=0)
    stack_ref[...] = stack
    put_pairs(half_sums(got, stack, 1), *outs)


def near_sums_kernel(count, stack_ref, *refs):
    got, (keep_ref, send_ref) = refs[:count], refs[-2:]
    put_pairs(half_sums(got, stack_ref[...], 0), keep_ref, send_ref)


def correlate(part_ref, blocks):
    length = part_ref.shape[1]
    chunk = CHUNK * ANG
    corr = None
    for c in range(length // chunk):
        at = slice(c * chunk, (c + 1) * chunk)
        part = part_ref[:, at].astype(f32)
        left = jnp.concatenate([turn(part, -STEP * PAIR * m) for m in range(ROT // PAIR)], axis=0).astype(bf16)
        cls = jnp.concatenate([b[:, at].astype(f32) for b in blocks], axis=0)
        right = jnp.concatenate([turn(cls, STEP * j).astype(bf16) for j in range(PAIR)], axis=0)
        more = lax.dot_general(left, right, (((1,), (1,)), ((), ())), preferred_element_type=f32)
        corr = more if corr is None else corr + more
    return corr


def weighted(corr, weights_ref, half):
    n = weights_ref.shape[0]
    wide = corr.shape[1]
    k = wide // PAIR
    cols = weights_ref.shape[1] - ROT * 2 * k
    total = None
    for m in range(ROT // PAIR):
        i, b = m // 2, m % 2
        first = cols + ((2 * i + half) * 2 + b) * wide
        w = weights_ref[:, first : first + wide].astype(f32)
        more = w * corr[m * n : (m + 1) * n]
        total = more if total is None else total + more
    out = total[:, :k]
    for j in range(1, PAIR):
        out = out + total[:, j * k : (j + 1) * k]
    return out


def guest_kernel(part_ref, packed_ref, *refs):
    *blocks, out_ref, own_ref = refs
    out_ref[...] = correlate(part_ref, blocks)
    own_ref[...] = packed_ref[...]


def near_scores_kernel(part_ref, weights_ref, *refs):
    *blocks, out_ref = refs
    out_ref[...] = weighted(correlate(part_ref, blocks), weights_ref, 0)


def scores_kernel(near_ref, back_ref, weights_ref, out_ref):
    groups = lax.axis_size("cls")
    far = weighted(back_ref[...], weights_ref, 1)
    out = jnp.concatenate([near_ref[...], far], axis=1)
    out_ref[...] = swap_blocks(out, lax.axis_index("cls"), out.shape[1] // groups, groups) / ROT


def on_device(particles, references, pose_weights, class_mask):
    n, length = particles.shape
    per = references.shape[0]
    k = class_mask.shape[1]
    dom, groups = lax.axis_size("dom"), lax.axis_size("cls")
    cols = length // dom
    last = groups // 2
    vmem = pl.BlockSpec(memory_space=pltpu.VMEM)

    def call(kernel, name, outs, ins, limit=VMEM_BYTES):
        return pl.pallas_call(
            kernel,
            out_shape=[jax.ShapeDtypeStruct(*o) for o in outs],
            in_specs=ins,
            out_specs=[vmem] * len(outs),
            compiler_params=pltpu.CompilerParams(vmem_limit_bytes=limit),
            name=name,
        )

    def after(x, other):
        return lax.optimization_barrier((x, other))[0]

    def across(x, bit):
        return lax.ppermute(x, "cls", [(c, c ^ bit) for c in range(groups)])

    def reduced(keep, send):
        bit = 1
        while bit < last:
            keep = keep + across(send, bit)
            bit *= 2
            if bit < last:
                pairs = keep.reshape(keep.shape[0] // 2, 2, per, cols)
                keep, send = pairs[:, 0], pairs[:, 1]
        return keep[0]

    blocks = {0: references}
    bit = last // 2
    while bit:
        blocks.update({s | bit: across(b, bit) for s, b in list(blocks.items())})
        bit //= 2
    near = [blocks[s] for s in range(last)]
    packed = call(
        pack_kernel,
        "pack",
        [((n, cols + ROT * k), bf16)] * dom,
        [vmem] * 3,
        limit=VMEM_MOST,
    )(particles, pose_weights, class_mask)
    packed = after(packed, near)
    got = [packed[0]]
    for s in range(dom - 1, 0, -1):
        x = packed[s]
        got.append(lax.ppermute(x, "dom", [(d, d ^ s) for d in range(dom)]))

    guests = across(particles, last)
    back, got[0] = call(
        guest_kernel,
        "guest_scores",
        [((n * ROT // PAIR, PAIR * k // 2), f32), (packed[0].shape, bf16)],
        [vmem] * (2 + last),
    )(guests, packed[0], *near)
    got = after(got, back)
    send_shape = (max(last // 2, 1), per, cols)
    stack, keep, send = call(
        functools.partial(far_sums_kernel, dom),
        "far_sums",
        [((n * dom * COARSE, cols), bf16), (send_shape, f32), (send_shape, f32)],
        [vmem] * dom,
    )(*got)
    back = across(after(back, send), last)
    leaving = reduced(keep, send)
    arriving = across(leaving, last)
    (near_scores,) = call(near_scores_kernel, "near_scores", [((n, k // 2), f32)], [vmem] * (2 + last))(
        after(particles, leaving), got[0], *near
    )
    stack = after(stack, (near_scores, back))

    keep, send = call(
        functools.partial(near_sums_kernel, dom), "near_sums", [(send_shape, f32)] * 2, [vmem] * (1 + dom)
    )(stack, *got)
    near_sums = reduced(keep, send)

    (scored,) = call(scores_kernel, "scores", [((n, k), f32)], [vmem] * 3)(near_scores, back, got[0])
    arriving = after(arriving, scored)
    class_sums = (near_sums + arriving) / math.sqrt(n * dom * groups * ROT)
    return (scored, class_sums)


def solution(mesh):
    return jax.shard_map(
        on_device,
        mesh=mesh,
        in_specs=(
            P(("dom", "cls"), None),
            P("cls", None),
            P(("dom", "cls"), None, None),
            P(("dom", "cls"), None),
        ),
        out_specs=(P(("dom", "cls"), None), P("cls", "dom")),
        check_vma=False,
    )
```

```python
import functools
import math

import jax
import jax.numpy as jnp
from jax import lax
from jax.experimental import pallas as pl
from jax.experimental.pallas import tpu as pltpu
from jax.sharding import PartitionSpec as P

CYCLES = 64
ANG = 256
ROT = 24
STEP = ANG // ROT
FINE = 4
COARSE = ROT // FINE
PAIR = 2
CHUNK = 4
LANES = 128
VMEM_BYTES = 48 * 1024 * 1024
VMEM_MOST = 65900000
f32 = jnp.float32
bf16 = jnp.bfloat16


def turn(x, shift):
    shift %= ANG
    if shift == 0:
        return x
    halves, rest = shift // LANES, shift % LANES
    lane = lax.broadcasted_iota(jnp.int32, (x.shape[0], LANES), 1)
    pieces = []
    for c in range(x.shape[1] // ANG):
        lo = x[:, c * ANG : c * ANG + LANES]
        hi = x[:, c * ANG + LANES : (c + 1) * ANG]
        if halves:
            lo, hi = hi, lo
        if rest:
            lo, hi = pltpu.roll(lo, rest, 1), pltpu.roll(hi, rest, 1)
            lo, hi = jnp.where(lane < rest, hi, lo), jnp.where(lane < rest, lo, hi)
        pieces += [lo, hi]
    return jnp.concatenate(pieces, axis=1)


def swap_blocks(x, me, block, blocks):
    lane = lax.broadcasted_iota(jnp.int32, x.shape, 1)
    width = x.shape[1]
    bit = 1
    while bit < blocks:
        g = block * bit
        upper = (lane // g) % 2 == 1
        swapped = jnp.where(upper, pltpu.roll(x, g, 1), pltpu.roll(x, width - g, 1))
        x = jnp.where((me // bit) % 2 == 1, swapped, x)
        bit *= 2
    return x


def pack_kernel(part_ref, pose_ref, mask_ref, *slots):
    cols = part_ref.shape[1] // len(slots)
    d, me, groups = lax.axis_index("dom"), lax.axis_index("cls"), lax.axis_size("cls")
    k = pose_ref.shape[2]
    half = k // 2
    for s, slot in enumerate(slots):
        slot[:, :cols] = part_ref[:, pl.ds(pl.multiple_of((d ^ s) * cols, cols), cols)]
    mask = mask_ref[...]
    for i in range(COARSE):
        fine = [pose_ref[:, FINE * i + j, :] * mask for j in range(FINE)]
        w = swap_blocks(jnp.concatenate(fine, axis=1).astype(f32), me, k // groups, groups)
        pieces = [w[:, j * k + h * half : j * k + (h + 1) * half] for h in range(2) for j in range(FINE)]
        w = jnp.concatenate(pieces, axis=1).astype(bf16)
        wide = w.shape[1]
        for slot in slots:
            slot[:, cols + i * wide : cols + (i + 1) * wide] = w


def rows_of(got, at):
    return jnp.concatenate([g[:, at].astype(f32) for g in got], axis=0)


def products(got, stack, half):
    cols = stack.shape[1]
    wide = (got[0].shape[1] - cols) // COARSE // 2
    at = [slice(cols + (2 * i + half) * wide, cols + (2 * i + half + 1) * wide) for i in range(COARSE)]
    w = jnp.concatenate([rows_of(got, a).astype(bf16) for a in at], axis=0)
    return lax.dot_general(w, stack, (((0,), (0,)), ((), ())), preferred_element_type=f32)


def turned_back(t):
    k = t.shape[0] // FINE
    total = t[:k]
    for j in range(1, FINE):
        total = total + turn(t[j * k : (j + 1) * k], -STEP * j)
    return total


def rotated(got, cols):
    part = rows_of(got, slice(0, cols))
    return jnp.concatenate([turn(part, -STEP * FINE * i).astype(bf16) for i in range(COARSE)], axis=0)


def put_pairs(total, keep_ref, send_ref):
    half, per, _ = keep_ref.shape
    for m in range(half):
        keep_ref[m] = total[2 * m * per : (2 * m + 1) * per]
        if total.shape[0] > per:
            send_ref[m] = total[(2 * m + 1) * per : (2 * m + 2) * per]


def early_sums_kernel(*refs):
    *got, stack_ref, out_ref = refs
    stack = rotated(got, stack_ref.shape[1])
    stack_ref[...] = stack
    out_ref[...] = products(got, stack, 1)


def far_sums_kernel(early_ref, *refs):
    *got, stack_ref, keep_ref, send_ref = refs
    stack = rotated(got, stack_ref.shape[1])
    stack_ref[...] = stack
    put_pairs(turned_back(early_ref[...] + products(got, stack, 1)), keep_ref, send_ref)


def near_sums_kernel(count, early_ref, late_ref, *refs):
    *got, keep_ref, send_ref = refs
    t = products(got[:count], early_ref[...], 0) + products(got[count:], late_ref[...], 0)
    put_pairs(turned_back(t), keep_ref, send_ref)


def correlate(part_ref, blocks):
    length = part_ref.shape[1]
    chunk = CHUNK * ANG
    corr = None
    for c in range(length // chunk):
        at = slice(c * chunk, (c + 1) * chunk)
        part = part_ref[:, at].astype(f32)
        left = jnp.concatenate([turn(part, -STEP * PAIR * m) for m in range(ROT // PAIR)], axis=0).astype(bf16)
        cls = jnp.concatenate([b[:, at].astype(f32) for b in blocks], axis=0)
        right = jnp.concatenate([turn(cls, STEP * j).astype(bf16) for j in range(PAIR)], axis=0)
        more = lax.dot_general(left, right, (((1,), (1,)), ((), ())), preferred_element_type=f32)
        corr = more if corr is None else corr + more
    return corr


def weighted(corr, weights_ref, half):
    n = weights_ref.shape[0]
    wide = corr.shape[1]
    k = wide // PAIR
    cols = weights_ref.shape[1] - ROT * 2 * k
    total = None
    for m in range(ROT // PAIR):
        i, b = m // 2, m % 2
        first = cols + ((2 * i + half) * 2 + b) * wide
        w = weights_ref[:, first : first + wide].astype(f32)
        more = w * corr[m * n : (m + 1) * n]
        total = more if total is None else total + more
    out = total[:, :k]
    for j in range(1, PAIR):
        out = out + total[:, j * k : (j + 1) * k]
    return out


def guest_kernel(part_ref, packed_ref, *refs):
    *blocks, out_ref, own_ref = refs
    out_ref[...] = correlate(part_ref, blocks)
    own_ref[...] = packed_ref[...]


def near_scores_kernel(part_ref, weights_ref, *refs):
    *blocks, out_ref = refs
    out_ref[...] = weighted(correlate(part_ref, blocks), weights_ref, 0)


def scores_kernel(near_ref, back_ref, weights_ref, out_ref):
    groups = lax.axis_size("cls")
    far = weighted(back_ref[...], weights_ref, 1)
    out = jnp.concatenate([near_ref[...], far], axis=1)
    out_ref[...] = swap_blocks(out, lax.axis_index("cls"), out.shape[1] // groups, groups) / ROT


def on_device(particles, references, pose_weights, class_mask):
    n, length = particles.shape
    per = references.shape[0]
    k = class_mask.shape[1]
    dom, groups = lax.axis_size("dom"), lax.axis_size("cls")
    cols = length // dom
    last = groups // 2
    vmem = pl.BlockSpec(memory_space=pltpu.VMEM)

    def call(kernel, name, outs, ins, limit=VMEM_BYTES):
        return pl.pallas_call(
            kernel,
            out_shape=[jax.ShapeDtypeStruct(*o) for o in outs],
            in_specs=ins,
            out_specs=[vmem] * len(outs),
            compiler_params=pltpu.CompilerParams(vmem_limit_bytes=limit),
            name=name,
        )

    def after(x, other):
        return lax.optimization_barrier((x, other))[0]

    def across(x, bit):
        return lax.ppermute(x, "cls", [(c, c ^ bit) for c in range(groups)])

    def reduced(keep, send):
        bit = 1
        while bit < last:
            keep = keep + across(send, bit)
            bit *= 2
            if bit < last:
                pairs = keep.reshape(keep.shape[0] // 2, 2, per, cols)
                keep, send = pairs[:, 0], pairs[:, 1]
        return keep[0]

    blocks = {0: references}
    bit = last // 2
    while bit:
        blocks.update({s | bit: across(b, bit) for s, b in list(blocks.items())})
        bit //= 2
    near = [blocks[s] for s in range(last)]
    packed = call(
        pack_kernel,
        "pack",
        [((n, cols + ROT * k), bf16)] * dom,
        [vmem] * 3,
        limit=VMEM_MOST,
    )(particles, pose_weights, class_mask)
    packed = after(packed, near)
    got = [packed[0]]
    for s in range(dom - 1, 0, -1):
        x = packed[s]
        got.append(lax.ppermute(x, "dom", [(d, d ^ s) for d in range(dom)]))

    guests = across(particles, last)
    back, got[0] = call(
        guest_kernel,
        "guest_scores",
        [((n * ROT // PAIR, PAIR * k // 2), f32), (packed[0].shape, bf16)],
        [vmem] * (2 + last),
    )(guests, packed[0], *near)
    send_shape = (max(last // 2, 1), per, cols)
    first = dom // 2
    early_stack, early = call(
        early_sums_kernel,
        "early_sums",
        [((n * first * COARSE, cols), bf16), ((FINE * k // 2, cols), f32)],
        [vmem] * first,
    )(*got[:first])
    got = got[:first] + after(got[first:], early)
    late_stack, keep, send = call(
        far_sums_kernel,
        "far_sums",
        [((n * (dom - first) * COARSE, cols), bf16), (send_shape, f32), (send_shape, f32)],
        [vmem] * (1 + dom - first),
    )(early, *got[first:])
    back = across(after(back, send), last)
    leaving = reduced(keep, send)
    arriving = across(leaving, last)
    (near_scores,) = call(near_scores_kernel, "near_scores", [((n, k // 2), f32)], [vmem] * (2 + last))(
        after(particles, leaving), got[0], *near
    )
    late_stack = after(late_stack, (near_scores, back))

    keep, send = call(
        functools.partial(near_sums_kernel, first), "near_sums", [(send_shape, f32)] * 2, [vmem] * (2 + dom)
    )(early_stack, late_stack, *got)
    near_sums = reduced(keep, send)

    (scored,) = call(scores_kernel, "scores", [((n, k), f32)], [vmem] * 3)(near_scores, back, got[0])
    arriving = after(arriving, scored)
    class_sums = (near_sums + arriving) / math.sqrt(n * dom * groups * ROT)
    return (scored, class_sums)


def solution(mesh):
    return jax.shard_map(
        on_device,
        mesh=mesh,
        in_specs=(
            P(("dom", "cls"), None),
            P("cls", None),
            P(("dom", "cls"), None, None),
            P(("dom", "cls"), None),
        ),
        out_specs=(P(("dom", "cls"), None), P("cls", "dom")),
        check_vma=False,
    )
```

```python
import functools
import math

import jax
import jax.numpy as jnp
from jax import lax
from jax.experimental import pallas as pl
from jax.experimental.pallas import tpu as pltpu
from jax.sharding import PartitionSpec as P

CYCLES = 64
ANG = 256
ROT = 24
STEP = ANG // ROT
FINE = 4
COARSE = ROT // FINE
PAIR = 2
CHUNK = 4
LANES = 128
VMEM_BYTES = 48 * 1024 * 1024
VMEM_MOST = 56000000
f32 = jnp.float32
bf16 = jnp.bfloat16


def turn(x, shift):
    shift %= ANG
    if shift == 0:
        return x
    halves, rest = shift // LANES, shift % LANES
    lane = lax.broadcasted_iota(jnp.int32, (x.shape[0], LANES), 1)
    pieces = []
    for c in range(x.shape[1] // ANG):
        lo = x[:, c * ANG : c * ANG + LANES]
        hi = x[:, c * ANG + LANES : (c + 1) * ANG]
        if halves:
            lo, hi = hi, lo
        if rest:
            lo, hi = pltpu.roll(lo, rest, 1), pltpu.roll(hi, rest, 1)
            lo, hi = jnp.where(lane < rest, hi, lo), jnp.where(lane < rest, lo, hi)
        pieces += [lo, hi]
    return jnp.concatenate(pieces, axis=1)


def swap_blocks(x, me, block, blocks):
    lane = lax.broadcasted_iota(jnp.int32, x.shape, 1)
    width = x.shape[1]
    bit = 1
    while bit < blocks:
        g = block * bit
        upper = (lane // g) % 2 == 1
        swapped = jnp.where(upper, pltpu.roll(x, g, 1), pltpu.roll(x, width - g, 1))
        x = jnp.where((me // bit) % 2 == 1, swapped, x)
        bit *= 2
    return x


def pack_kernel(part_ref, pose_ref, mask_ref, *slots):
    cols = part_ref.shape[1] // len(slots)
    d, me, groups = lax.axis_index("dom"), lax.axis_index("cls"), lax.axis_size("cls")
    k = pose_ref.shape[2]
    half = k // 2
    for s, slot in enumerate(slots):
        slot[:, :cols] = part_ref[:, pl.ds(pl.multiple_of((d ^ s) * cols, cols), cols)]
    mask = mask_ref[...]
    for i in range(COARSE):
        fine = [pose_ref[:, FINE * i + j, :] * mask for j in range(FINE)]
        w = swap_blocks(jnp.concatenate(fine, axis=1).astype(f32), me, k // groups, groups)
        pieces = [w[:, j * k + h * half : j * k + (h + 1) * half] for h in range(2) for j in range(FINE)]
        w = jnp.concatenate(pieces, axis=1).astype(bf16)
        wide = w.shape[1]
        for slot in slots:
            slot[:, cols + i * wide : cols + (i + 1) * wide] = w


def rows_of(got, at):
    return jnp.concatenate([g[:, at].astype(f32) for g in got], axis=0)


def products(got, stack, half):
    cols = stack.shape[1]
    wide = (got[0].shape[1] - cols) // COARSE // 2
    at = [slice(cols + (2 * i + half) * wide, cols + (2 * i + half + 1) * wide) for i in range(COARSE)]
    w = jnp.concatenate([rows_of(got, a).astype(bf16) for a in at], axis=0)
    return lax.dot_general(w, stack, (((0,), (0,)), ((), ())), preferred_element_type=f32)


def turned_back(t):
    k = t.shape[0] // FINE
    total = t[:k]
    for j in range(1, FINE):
        total = total + turn(t[j * k : (j + 1) * k], -STEP * j)
    return total


def rotated(got, cols):
    part = rows_of(got, slice(0, cols))
    return jnp.concatenate([turn(part, -STEP * FINE * i).astype(bf16) for i in range(COARSE)], axis=0)


def put_pairs(total, keep_ref, send_ref):
    half, per, _ = keep_ref.shape
    for m in range(half):
        keep_ref[m] = total[2 * m * per : (2 * m + 1) * per]
        if total.shape[0] > per:
            send_ref[m] = total[(2 * m + 1) * per : (2 * m + 2) * per]


def early_sums_kernel(*refs):
    *got, stack_ref, out_ref = refs
    stack = rotated(got, stack_ref.shape[1])
    stack_ref[...] = stack
    out_ref[...] = products(got, stack, 1)


def far_sums_kernel(early_ref, *refs):
    *got, stack_ref, keep_ref, send_ref = refs
    stack = rotated(got, stack_ref.shape[1])
    stack_ref[...] = stack
    put_pairs(turned_back(early_ref[...] + products(got, stack, 1)), keep_ref, send_ref)


def near_sums_kernel(count, early_ref, late_ref, *refs):
    *got, keep_ref, send_ref = refs
    t = products(got[:count], early_ref[...], 0) + products(got[count:], late_ref[...], 0)
    put_pairs(turned_back(t), keep_ref, send_ref)


def correlate(part_ref, blocks):
    length = part_ref.shape[1]
    chunk = CHUNK * ANG
    corr = None
    for c in range(length // chunk):
        at = slice(c * chunk, (c + 1) * chunk)
        part = part_ref[:, at].astype(f32)
        left = jnp.concatenate([turn(part, -STEP * PAIR * m) for m in range(ROT // PAIR)], axis=0).astype(bf16)
        cls = jnp.concatenate([b[:, at].astype(f32) for b in blocks], axis=0)
        right = jnp.concatenate([turn(cls, STEP * j).astype(bf16) for j in range(PAIR)], axis=0)
        more = lax.dot_general(left, right, (((1,), (1,)), ((), ())), preferred_element_type=f32)
        corr = more if corr is None else corr + more
    return corr


def weighted(corr, weights_ref, half):
    n = weights_ref.shape[0]
    wide = corr.shape[1]
    k = wide // PAIR
    cols = weights_ref.shape[1] - ROT * 2 * k
    total = None
    for m in range(ROT // PAIR):
        i, b = m // 2, m % 2
        first = cols + ((2 * i + half) * 2 + b) * wide
        w = weights_ref[:, first : first + wide].astype(f32)
        more = w * corr[m * n : (m + 1) * n]
        total = more if total is None else total + more
    out = total[:, :k]
    for j in range(1, PAIR):
        out = out + total[:, j * k : (j + 1) * k]
    return out


def guest_kernel(part_ref, packed_ref, *refs):
    *blocks, out_ref, own_ref = refs
    out_ref[...] = correlate(part_ref, blocks)
    own_ref[...] = packed_ref[...]


def near_scores_kernel(part_ref, weights_ref, *refs):
    *blocks, out_ref = refs
    out_ref[...] = weighted(correlate(part_ref, blocks), weights_ref, 0)


def scores_kernel(near_ref, back_ref, weights_ref, out_ref):
    groups = lax.axis_size("cls")
    far = weighted(back_ref[...], weights_ref, 1)
    out = jnp.concatenate([near_ref[...], far], axis=1)
    out_ref[...] = swap_blocks(out, lax.axis_index("cls"), out.shape[1] // groups, groups) / ROT


def on_device(particles, references, pose_weights, class_mask):
    n, length = particles.shape
    per = references.shape[0]
    k = class_mask.shape[1]
    dom, groups = lax.axis_size("dom"), lax.axis_size("cls")
    cols = length // dom
    last = groups // 2
    vmem = pl.BlockSpec(memory_space=pltpu.VMEM)

    def call(kernel, name, outs, ins, limit=VMEM_BYTES):
        return pl.pallas_call(
            kernel,
            out_shape=[jax.ShapeDtypeStruct(*o) for o in outs],
            in_specs=ins,
            out_specs=[vmem] * len(outs),
            compiler_params=pltpu.CompilerParams(vmem_limit_bytes=limit),
            name=name,
        )

    def after(x, other):
        return lax.optimization_barrier((x, other))[0]

    def across(x, bit):
        return lax.ppermute(x, "cls", [(c, c ^ bit) for c in range(groups)])

    def reduced(keep, send):
        bit = 1
        while bit < last:
            keep = keep + across(send, bit)
            bit *= 2
            if bit < last:
                pairs = keep.reshape(keep.shape[0] // 2, 2, per, cols)
                keep, send = pairs[:, 0], pairs[:, 1]
        return keep[0]

    blocks = {0: references}
    bit = last // 2
    while bit:
        blocks.update({s | bit: across(b, bit) for s, b in list(blocks.items())})
        bit //= 2
    near = [blocks[s] for s in range(last)]
    packed = call(
        pack_kernel,
        "pack",
        [((n, cols + ROT * k), bf16)] * dom,
        [vmem] * 3,
        limit=VMEM_MOST,
    )(particles, pose_weights, class_mask)
    packed = after(packed, near)
    got = [packed[0]]
    for s in range(dom - 1, 0, -1):
        x = packed[s]
        got.append(lax.ppermute(x, "dom", [(d, d ^ s) for d in range(dom)]))

    guests = across(particles, last)
    back, got[0] = call(
        guest_kernel,
        "guest_scores",
        [((n * ROT // PAIR, PAIR * k // 2), f32), (packed[0].shape, bf16)],
        [vmem] * (2 + last),
    )(guests, packed[0], *near)
    send_shape = (max(last // 2, 1), per, cols)
    first = dom // 2
    early_stack, early = call(
        early_sums_kernel,
        "early_sums",
        [((n * first * COARSE, cols), bf16), ((FINE * k // 2, cols), f32)],
        [vmem] * first,
    )(*got[:first])
    got = got[:first] + after(got[first:], early)
    late_stack, keep, send = call(
        far_sums_kernel,
        "far_sums",
        [((n * (dom - first) * COARSE, cols), bf16), (send_shape, f32), (send_shape, f32)],
        [vmem] * (1 + dom - first),
    )(early, *got[first:])
    back = across(after(back, send), last)
    leaving = reduced(keep, send)
    arriving = across(leaving, last)
    (near_scores,) = call(near_scores_kernel, "near_scores", [((n, k // 2), f32)], [vmem] * (2 + last))(
        after(particles, leaving), got[0], *near
    )
    late_stack = after(late_stack, (near_scores, back))

    keep, send = call(
        functools.partial(near_sums_kernel, first), "near_sums", [(send_shape, f32)] * 2, [vmem] * (2 + dom)
    )(early_stack, late_stack, *got)
    near_sums = reduced(keep, send)

    (scored,) = call(scores_kernel, "scores", [((n, k), f32)], [vmem] * 3)(near_scores, back, got[0])
    arriving = after(arriving, scored)
    class_sums = (near_sums + arriving) / math.sqrt(n * dom * groups * ROT)
    return (scored, class_sums)


def solution(mesh):
    return jax.shard_map(
        on_device,
        mesh=mesh,
        in_specs=(
            P(("dom", "cls"), None),
            P("cls", None),
            P(("dom", "cls"), None, None),
            P(("dom", "cls"), None),
        ),
        out_specs=(P(("dom", "cls"), None), P("cls", "dom")),
        check_vma=False,
    )
```

```python
import functools
import math

import jax
import jax.numpy as jnp
from jax import lax
from jax.experimental import pallas as pl
from jax.experimental.pallas import tpu as pltpu
from jax.sharding import PartitionSpec as P

CYCLES = 64
ANG = 256
ROT = 24
STEP = ANG // ROT
FINE = 4
COARSE = ROT // FINE
PAIR = 2
CHUNK = 4
LANES = 128
VMEM_BYTES = 48 * 1024 * 1024
VMEM_MOST = 56000000
f32 = jnp.float32
bf16 = jnp.bfloat16


def turn(x, shift):
    shift %= ANG
    if shift == 0:
        return x
    halves, rest = shift // LANES, shift % LANES
    lane = lax.broadcasted_iota(jnp.int32, (x.shape[0], LANES), 1)
    pieces = []
    for c in range(x.shape[1] // ANG):
        lo = x[:, c * ANG : c * ANG + LANES]
        hi = x[:, c * ANG + LANES : (c + 1) * ANG]
        if halves:
            lo, hi = hi, lo
        if rest:
            lo, hi = pltpu.roll(lo, rest, 1), pltpu.roll(hi, rest, 1)
            lo, hi = jnp.where(lane < rest, hi, lo), jnp.where(lane < rest, lo, hi)
        pieces += [lo, hi]
    return jnp.concatenate(pieces, axis=1)


def swap_blocks(x, me, block, blocks):
    lane = lax.broadcasted_iota(jnp.int32, x.shape, 1)
    width = x.shape[1]
    bit = 1
    while bit < blocks:
        g = block * bit
        upper = (lane // g) % 2 == 1
        swapped = jnp.where(upper, pltpu.roll(x, g, 1), pltpu.roll(x, width - g, 1))
        x = jnp.where((me // bit) % 2 == 1, swapped, x)
        bit *= 2
    return x


def pack_kernel(part_ref, pose_ref, mask_ref, *slots):
    cols = part_ref.shape[1] // len(slots)
    d, me, groups = lax.axis_index("dom"), lax.axis_index("cls"), lax.axis_size("cls")
    k = pose_ref.shape[2]
    half = k // 2
    for s, slot in enumerate(slots):
        slot[:, :cols] = part_ref[:, pl.ds(pl.multiple_of((d ^ s) * cols, cols), cols)]
    mask = mask_ref[...]
    for i in range(COARSE):
        fine = [pose_ref[:, FINE * i + j, :] * mask for j in range(FINE)]
        w = swap_blocks(jnp.concatenate(fine, axis=1).astype(f32), me, k // groups, groups)
        pieces = [w[:, j * k + h * half : j * k + (h + 1) * half] for h in range(2) for j in range(FINE)]
        w = jnp.concatenate(pieces, axis=1).astype(bf16)
        wide = w.shape[1]
        for slot in slots:
            slot[:, cols + i * wide : cols + (i + 1) * wide] = w


def rows_of(got, at):
    return jnp.concatenate([g[:, at].astype(f32) for g in got], axis=0)


def products(got, stack, half):
    cols = stack.shape[1]
    wide = (got[0].shape[1] - cols) // COARSE // 2
    at = [slice(cols + (2 * i + half) * wide, cols + (2 * i + half + 1) * wide) for i in range(COARSE)]
    w = jnp.concatenate([rows_of(got, a).astype(bf16) for a in at], axis=0)
    return lax.dot_general(w, stack, (((0,), (0,)), ((), ())), preferred_element_type=f32)


def turned_back(t):
    k = t.shape[0] // FINE
    total = t[:k]
    for j in range(1, FINE):
        total = total + turn(t[j * k : (j + 1) * k], -STEP * j)
    return total


def rotated(got, cols):
    part = rows_of(got, slice(0, cols))
    return jnp.concatenate([turn(part, -STEP * FINE * i).astype(bf16) for i in range(COARSE)], axis=0)


def put_pairs(total, keep_ref, send_ref):
    half, per, _ = keep_ref.shape
    for m in range(half):
        keep_ref[m] = total[2 * m * per : (2 * m + 1) * per]
        if total.shape[0] > per:
            send_ref[m] = total[(2 * m + 1) * per : (2 * m + 2) * per]


def early_sums_kernel(*refs):
    *got, stack_ref, out_ref = refs
    stack = rotated(got, stack_ref.shape[1])
    stack_ref[...] = stack
    out_ref[...] = products(got, stack, 1)


def far_sums_kernel(early_ref, *refs):
    *got, stack_ref, keep_ref, send_ref = refs
    stack = rotated(got, stack_ref.shape[1])
    stack_ref[...] = stack
    put_pairs(turned_back(early_ref[...] + products(got, stack, 1)), keep_ref, send_ref)


def near_sums_kernel(count, early_ref, late_ref, *refs):
    *got, keep_ref, send_ref = refs
    t = products(got[:count], early_ref[...], 0) + products(got[count:], late_ref[...], 0)
    put_pairs(turned_back(t), keep_ref, send_ref)


def correlate(part_ref, blocks):
    length = part_ref.shape[1]
    chunk = CHUNK * ANG
    corr = None
    for c in range(length // chunk):
        at = slice(c * chunk, (c + 1) * chunk)
        part = part_ref[:, at].astype(f32)
        left = jnp.concatenate([turn(part, -STEP * PAIR * m) for m in range(ROT // PAIR)], axis=0).astype(bf16)
        cls = jnp.concatenate([b[:, at].astype(f32) for b in blocks], axis=0)
        right = jnp.concatenate([turn(cls, STEP * j).astype(bf16) for j in range(PAIR)], axis=0)
        more = lax.dot_general(left, right, (((1,), (1,)), ((), ())), preferred_element_type=f32)
        corr = more if corr is None else corr + more
    return corr


def weighted(corr, weights_ref, half):
    n = weights_ref.shape[0]
    wide = corr.shape[1]
    k = wide // PAIR
    cols = weights_ref.shape[1] - ROT * 2 * k
    total = None
    for m in range(ROT // PAIR):
        i, b = m // 2, m % 2
        first = cols + ((2 * i + half) * 2 + b) * wide
        w = weights_ref[:, first : first + wide].astype(f32)
        more = w * corr[m * n : (m + 1) * n]
        total = more if total is None else total + more
    out = total[:, :k]
    for j in range(1, PAIR):
        out = out + total[:, j * k : (j + 1) * k]
    return out


def guest_kernel(part_ref, *refs):
    *blocks, out_ref = refs
    out_ref[...] = correlate(part_ref, blocks)


def near_scores_kernel(part_ref, weights_ref, *refs):
    *blocks, out_ref = refs
    out_ref[...] = weighted(correlate(part_ref, blocks), weights_ref, 0)


def scores_kernel(near_ref, back_ref, weights_ref, out_ref):
    groups = lax.axis_size("cls")
    far = weighted(back_ref[...], weights_ref, 1)
    out = jnp.concatenate([near_ref[...], far], axis=1)
    out_ref[...] = swap_blocks(out, lax.axis_index("cls"), out.shape[1] // groups, groups) / ROT


def on_device(particles, references, pose_weights, class_mask):
    n, length = particles.shape
    per = references.shape[0]
    k = class_mask.shape[1]
    dom, groups = lax.axis_size("dom"), lax.axis_size("cls")
    cols = length // dom
    last = groups // 2
    vmem = pl.BlockSpec(memory_space=pltpu.VMEM)

    def call(kernel, name, outs, ins, limit=VMEM_BYTES):
        return pl.pallas_call(
            kernel,
            out_shape=[jax.ShapeDtypeStruct(*o) for o in outs],
            in_specs=ins,
            out_specs=[vmem] * len(outs),
            compiler_params=pltpu.CompilerParams(vmem_limit_bytes=limit),
            name=name,
        )

    def after(x, other):
        return lax.optimization_barrier((x, other))[0]

    def across(x, bit):
        return lax.ppermute(x, "cls", [(c, c ^ bit) for c in range(groups)])

    def reduced(keep, send):
        bit = 1
        while bit < last:
            keep = keep + across(send, bit)
            bit *= 2
            if bit < last:
                pairs = keep.reshape(keep.shape[0] // 2, 2, per, cols)
                keep, send = pairs[:, 0], pairs[:, 1]
        return keep[0]

    blocks = {0: references}
    bit = last // 2
    while bit:
        blocks.update({s | bit: across(b, bit) for s, b in list(blocks.items())})
        bit //= 2
    near = [blocks[s] for s in range(last)]
    packed = call(
        pack_kernel,
        "pack",
        [((n, cols + ROT * k), bf16)] * dom,
        [vmem] * 3,
        limit=VMEM_MOST,
    )(particles, pose_weights, class_mask)
    packed = after(packed, near)
    got = [packed[0]]
    for s in range(dom - 1, 0, -1):
        x = packed[s]
        got.append(lax.ppermute(x, "dom", [(d, d ^ s) for d in range(dom)]))

    guests = across(particles, last)
    (back,) = call(
        guest_kernel,
        "guest_scores",
        [((n * ROT // PAIR, PAIR * k // 2), f32)],
        [vmem] * (1 + last),
    )(guests, *near)
    send_shape = (max(last // 2, 1), per, cols)
    first = dom // 2
    early_stack, early = call(
        early_sums_kernel,
        "early_sums",
        [((n * first * COARSE, cols), bf16), ((FINE * k // 2, cols), f32)],
        [vmem] * first,
    )(*got[:first])
    got = got[:first] + after(got[first:], (early, back))
    late_stack, keep, send = call(
        far_sums_kernel,
        "far_sums",
        [((n * (dom - first) * COARSE, cols), bf16), (send_shape, f32), (send_shape, f32)],
        [vmem] * (1 + dom - first),
    )(early, *got[first:])
    back = across(after(back, send), last)
    leaving = reduced(keep, send)
    arriving = across(leaving, last)
    (near_scores,) = call(near_scores_kernel, "near_scores", [((n, k // 2), f32)], [vmem] * (2 + last))(
        after(particles, leaving), got[0], *near
    )
    late_stack = after(late_stack, (near_scores, back))

    keep, send = call(
        functools.partial(near_sums_kernel, first), "near_sums", [(send_shape, f32)] * 2, [vmem] * (2 + dom)
    )(early_stack, late_stack, *got)
    near_sums = reduced(keep, send)

    (scored,) = call(scores_kernel, "scores", [((n, k), f32)], [vmem] * 3)(near_scores, back, got[0])
    arriving = after(arriving, scored)
    class_sums = (near_sums + arriving) / math.sqrt(n * dom * groups * ROT)
    return (scored, class_sums)


def solution(mesh):
    return jax.shard_map(
        on_device,
        mesh=mesh,
        in_specs=(
            P(("dom", "cls"), None),
            P("cls", None),
            P(("dom", "cls"), None, None),
            P(("dom", "cls"), None),
        ),
        out_specs=(P(("dom", "cls"), None), P("cls", "dom")),
        check_vma=False,
    )
```
